256 devices in a mesh: section: 8 (over x, z_hi), ctx: 32 (over y, z_lo, core).
Axes of the slice: x: 4, y: 4, z: 8 (z_hi: 2, z_lo: 4; z = z_hi * 4 + z_lo), core: 2. Of those that a mesh axis runs over, the one named last changes fastest.
Arguments:
- hidden: bfloat16 [8, 8192, 4096], P('section', 'ctx'), may hold values from -6 to 6
- query: bfloat16 [8, 8192, 2048], P('section', 'ctx'), may hold values from -480 to 480
- keyv: bfloat16 [8, 8192, 2048], P('section', 'ctx'), may hold values from -6 to 6
- value: bfloat16 [8, 8192, 2048], P('section', 'ctx'), may hold values from -6 to 6
- segments: int32 [8, 8192], P('section', 'ctx'), may hold values from 0 to 15, as said below
- out_weight: bfloat16 [8, 2048, 4096], P('section', 'ctx'), may hold values from -0.125 to 0.125
Outputs:
- passed: bfloat16 [8, 8192, 4096], P('section', 'ctx')
The draws below stay inside these ranges and needn't reach their ends.
Inputs may be any that keep to these rules, and one draw needn't show every extreme that they name: `segments`: within each micro-batch the numbers never fall along the tokens and each of 0 to 15 names one document of 256 to 768 tokens; in every micro-batch at least one document has exactly 768 tokens.
All inputs are finite; a program needn't handle non-finite values.
Results may differ from the reference program's by a relative error of at most 0.0085.
Values may be sent and summed in bfloat16 or wider, within the bound.
No kernel may reach another device: no remote copies, remote signals or barrier semaphores. Data moves between devices by JAX's collectives and lax.ppermute only.
A program may use at most 192 MiB of HBM per device.

```python
import jax
import jax.numpy as jnp
from jax import lax

D = 4096
HEADS = 16
DH = 128
TOK_DEV = 256
SPAN = 3
MICRO = 8
TOKENS = 8192


def shuffle_rows(key, table):
    rows, width = table.shape
    scores = jax.random.randint(key, (rows, width), 0, 1 << 20) * width + jnp.arange(width, dtype=jnp.int32)[None, :]
    order = jnp.argsort(scores, axis=1, stable=True).astype(jnp.int32)
    return jnp.take_along_axis(table, order, axis=1)


def draw_segments(key, part):
    key = jax.random.fold_in(key, 11)
    first, second, third, fourth = jax.random.split(key, 4)
    count = TOKENS // (2 * TOK_DEV)
    half_count = count // 2
    offsets = jax.random.randint(first, (MICRO, half_count), -TOK_DEV, TOK_DEV + 1)
    picked = jax.random.randint(second, (MICRO, 1), 0, half_count)
    places = jnp.arange(half_count, dtype=jnp.int32)[None, :]
    offsets = jnp.where(places == picked, (SPAN - 2) * TOK_DEV, offsets).astype(jnp.int32)
    mirrored = shuffle_rows(third, -offsets)
    middle = jnp.zeros((MICRO, count - 2 * half_count), jnp.int32)
    whole = jnp.concatenate([offsets, middle, mirrored], axis=1)
    whole = shuffle_rows(fourth, whole)
    lengths = (2 * TOK_DEV + whole).astype(jnp.int32)
    cuts = jnp.cumsum(lengths, axis=1).astype(jnp.int32)
    inner = cuts[:, 0:count - 1]
    positions = jnp.arange(TOKENS, dtype=jnp.int32)
    above = positions[None, :, None] >= inner[:, None, :]
    return jnp.sum(above.astype(jnp.int32), axis=-1).astype(jnp.int32)


def draw_query(key, part):
    key = jax.random.fold_in(key, 7)
    first = jax.random.fold_in(key, 0)
    base = jnp.clip(jax.random.normal(first, (MICRO, TOKENS, HEADS * DH), jnp.float32), -6.0, 6.0)
    return base.astype(jnp.bfloat16)


def shard_levels(stream_key, extent, shards, smallest, top_value):
    loudness, own = 1.0, jax.random.fold_in(stream_key, 6)
    for position, blocks in shards:
        heights = jnp.exp(jax.random.uniform(jax.random.fold_in(own, position), (blocks,), jnp.float32, smallest / len(shards), top_value / len(shards)))
        loudness = loudness * jnp.repeat(heights, extent[position] // blocks).reshape([-1 if axis == position else 1 for axis in range(len(extent))])
    return loudness


def normal_values(own_key, shape, scale, bound, shards=(), held_as=jnp.bfloat16):
    level = shard_levels(own_key, shape, shards, -0.22, 0.18) if shards else 1.0
    values = jax.random.normal(own_key, shape, jnp.float32) * scale * level
    return jnp.minimum(jnp.maximum(values, -bound), bound).astype(held_as)


def setup_inputs(seed: int = 0) -> dict:
    key_list = jax.random.split(jax.random.key(seed), 7)
    return {
        "hidden": normal_values(key_list[0], (MICRO, TOKENS, D), 1.0, 6.0, ((0, 8), (1, 32))),
        "query": draw_query(jax.random.fold_in(key_list[6], 71), 0),
        "keyv": normal_values(key_list[2], (MICRO, TOKENS, HEADS * DH), 1.0, 6.0, ((0, 8), (1, 32))),
        "value": normal_values(key_list[3], (MICRO, TOKENS, HEADS * DH), 1.0, 6.0, ((0, 8), (1, 32))),
        "segments": draw_segments(jax.random.fold_in(key_list[6], 71), 0),
        "out_weight": normal_values(key_list[5], (MICRO, HEADS * DH, D), (HEADS * DH) ** -0.5, 0.125, ((0, 8), (1, 32))),
    }


def layer(state, queries, keys, values, labels, out_matrix):
    resid = state.astype(jnp.float32)
    rows = resid.shape[0]
    query_rows = queries.reshape(rows, HEADS, DH)
    key_rows = keys.reshape(rows, HEADS, DH)
    value_rows = values.reshape(rows, HEADS, DH)
    margin = SPAN * TOK_DEV
    key_pad = jnp.pad(key_rows, ((margin, margin), (0, 0), (0, 0)))
    value_pad = jnp.pad(value_rows, ((margin, margin), (0, 0), (0, 0)))
    label_pad = jnp.pad(labels, (margin, margin))
    inv_scale = 1.0 / (DH ** 0.5)
    reach = (2 * SPAN + 1) * TOK_DEV

    def one_block(index):
        start = (index * TOK_DEV).astype(jnp.int32)
        query_part = lax.dynamic_slice_in_dim(query_rows, start, TOK_DEV, 0).astype(jnp.float32)
        key_part = lax.dynamic_slice_in_dim(key_pad, start, reach, 0).astype(jnp.float32)
        value_part = lax.dynamic_slice_in_dim(value_pad, start, reach, 0).astype(jnp.float32)
        own_labels = lax.dynamic_slice_in_dim(labels, start, TOK_DEV, 0)
        far_labels = lax.dynamic_slice_in_dim(label_pad, start, reach, 0)
        match = own_labels[:, None] == far_labels[None, :]
        scores = jnp.einsum("qhd,khd->hqk", query_part, key_part) * inv_scale
        scores = jnp.where(match[None], scores, -1e30)
        top = jnp.max(scores, axis=2, keepdims=True)
        expo = jnp.exp(scores - top)
        probs = (expo / jnp.sum(expo, axis=2, keepdims=True)).astype(jnp.bfloat16)
        return jnp.einsum("hqk,khd->qhd", probs.astype(jnp.float32), value_part).astype(jnp.bfloat16)

    count = rows // TOK_DEV
    attended = lax.map(one_block, jnp.arange(count, dtype=jnp.int32))
    attended = attended.reshape(rows, HEADS * DH)
    output = jnp.dot(attended, out_matrix, preferred_element_type=jnp.float32)
    return (resid + output).astype(jnp.bfloat16)


def reference(hidden, query, keyv, value, segments, out_weight):
    results = []
    for section_index in range(MICRO):
        results.append(layer(hidden[section_index], query[section_index], keyv[section_index], value[section_index], segments[section_index] + 1, out_weight[section_index]))
    stacked = jnp.stack(results, axis=0)
    return jnp.roll(stacked, 1, axis=0)
```

```python
import functools

import jax
import jax.numpy as jnp
from jax import lax
from jax.experimental import pallas as pl
from jax.experimental.pallas import tpu as pltpu
from jax.sharding import Mesh, PartitionSpec as P

DH = 128
SPAN = 3
BLK = 256
LINE = 8
PAIR = 256
REACH = 2 * SPAN + 1
BLOCKS = LINE + 2 * SPAN
MARK = 16
LOG2E = 1.4426950408889634
WINDOWS = (2, 3, 4, 5, 7)
PARTS = 2
CHIPS = LINE // 2
MIB = 1024 * 1024


ANY = pl.BlockSpec(memory_space=pl.ANY)
WHOLE = pl.BlockSpec(memory_space=pltpu.VMEM)
SCALARS = pl.BlockSpec(memory_space=pltpu.SMEM)


def run_copies(pairs, sems):
    copies = [pltpu.make_async_copy(src, dst, sems.at[index]) for index, (src, dst) in enumerate(pairs)]
    for copy in copies:
        copy.start()
    for copy in copies:
        copy.wait()


def pack_body(here_ref, *refs):
    arrays, mine_ref, other_ref = refs[:-2], refs[-2], refs[-1]
    chip, core = here_ref[0], here_ref[1]
    for j in range(LINE):

        def store(out_ref, j=j):
            for index, ref in enumerate(arrays):
                if ref.shape[0] == BLK:
                    piece = ref[:, j * PAIR : (j + 1) * PAIR]
                    out_ref[(j // 2) ^ chip, index * BLK : (index + 1) * BLK] = piece
                else:
                    labels = (ref[...] + 1).astype(jnp.float32)
                    out_ref[(j // 2) ^ chip, index * BLK :] = jnp.broadcast_to(labels, (MARK, BLK)).astype(jnp.bfloat16)

        pl.when(core == j % 2)(functools.partial(store, mine_ref))
        pl.when(core != j % 2)(functools.partial(store, other_ref))


def pack(here, *arrays):
    height = sum(BLK if array.shape[0] == BLK else MARK for array in arrays)
    out = jax.ShapeDtypeStruct((CHIPS, height, PAIR), jnp.bfloat16)
    return pl.pallas_call(
        pack_body,
        in_specs=[SCALARS] + [WHOLE] * len(arrays),
        out_specs=[WHOLE, WHOLE],
        out_shape=[out, out],
        compiler_params=pltpu.CompilerParams(vmem_limit_bytes=16 * MIB),
        cost_estimate=pl.CostEstimate(flops=0, bytes_accessed=2 * MIB, transcendentals=0),
        name="pack",
    )(here, *arrays)


def combine_body(mine_ref, got_ref, *refs):
    outs, sems = refs[:-1], refs[-1]
    run_copies(
        [(ref.at[k + 1], out.at[s]) for k, out in enumerate(outs) for s, ref in enumerate((mine_ref, got_ref))], sems
    )


def combine(mine, got):
    out = jax.ShapeDtypeStruct((2, *mine.shape[1:]), jnp.bfloat16)
    return pl.pallas_call(
        combine_body,
        in_specs=[ANY] * 2,
        out_specs=[ANY] * (CHIPS - 1),
        out_shape=[out] * (CHIPS - 1),
        scratch_shapes=[pltpu.SemaphoreType.DMA((2 * (CHIPS - 1),))],
        compiler_params=pltpu.CompilerParams(vmem_limit_bytes=4 * MIB),
        cost_estimate=pl.CostEstimate(flops=0, bytes_accessed=2 * MIB, transcendentals=0),
        name="combine",
    )(mine, got)


def assemble_body(here_ref, mine_ref, got_ref, *refs):
    far, out_ref, sems = refs[:-2], refs[-2], refs[-1]
    chip, core = here_ref[0], here_ref[1]
    pairs = [(mine_ref.at[0], out_ref.at[2 * chip + core]), (got_ref.at[0], out_ref.at[2 * chip + 1 - core])]
    for k, ref in enumerate(far):
        place = 2 * (chip ^ (k + 1))
        pairs += [(ref.at[0], out_ref.at[place + core]), (ref.at[1], out_ref.at[place + 1 - core])]
    run_copies(pairs, sems)


def assemble(here, mine, got, far):
    return pl.pallas_call(
        assemble_body,
        in_specs=[SCALARS] + [ANY] * (1 + CHIPS),
        out_specs=ANY,
        out_shape=jax.ShapeDtypeStruct((LINE, *mine.shape[1:]), jnp.bfloat16),
        scratch_shapes=[pltpu.SemaphoreType.DMA((LINE,))],
        compiler_params=pltpu.CompilerParams(vmem_limit_bytes=4 * MIB),
        cost_estimate=pl.CostEstimate(flops=0, bytes_accessed=2 * MIB, transcendentals=0),
        name="assemble",
    )(here, mine, got, *far)


def divide_body(here_ref, near_ref, *refs):
    far, own_ref, send_ref, sems = refs[:-3], refs[-3], refs[-2], refs[-1]
    core = here_ref[1]
    pairs = []
    for k, ref in enumerate((near_ref.at[0], *far)):
        pairs += [(ref.at[core], own_ref.at[k]), (ref.at[1 - core], send_ref.at[k])]
    run_copies(pairs, sems)


def divide(here, near, far):
    out = jax.ShapeDtypeStruct((CHIPS, BLK, PAIR), jnp.bfloat16)
    return pl.pallas_call(
        divide_body,
        in_specs=[SCALARS] + [ANY] * CHIPS,
        out_specs=[ANY, ANY],
        out_shape=[out, out],
        scratch_shapes=[pltpu.SemaphoreType.DMA((LINE,))],
        compiler_params=pltpu.CompilerParams(vmem_limit_bytes=4 * MIB),
        cost_estimate=pl.CostEstimate(flops=0, bytes_accessed=2 * MIB, transcendentals=0),
        name="divide",
    )(here, near, *far)


def attention_body(here_ref, query_ref, left_ref, kv_ref, right_ref, out_ref, keys, values, labels, sems):
    step = pl.program_id(0)

    @pl.when(step == 0)
    def _():
        pairs = []
        for dst, first, rows in ((keys, 0, BLK), (values, BLK, BLK), (labels, 2 * BLK, MARK)):
            at = 0
            for src, count in ((left_ref, SPAN), (kv_ref, LINE), (right_ref, SPAN)):
                pairs.append((src.at[:, pl.ds(first, rows)], dst.at[pl.ds(at, count)]))
                at += count
        run_copies(pairs, sems)

    own = jnp.max(labels[step + SPAN].astype(jnp.float32), axis=0, keepdims=True)
    first, last = jnp.min(own), jnp.max(own)
    marks = jnp.max(labels[...].astype(jnp.float32), axis=1)
    top, low = jnp.max(marks, axis=1, keepdims=True), jnp.min(marks, axis=1, keepdims=True)
    place = lax.broadcasted_iota(jnp.int32, (BLOCKS, 1), 0)
    beyond = (place >= SPAN + LINE) & (top == 0.0)
    before = jnp.where((top < first) & ~beyond, 1.0, 0.0)
    until = jnp.where((low <= last) & ~beyond, 1.0, 0.0)
    start = jnp.maximum(jnp.sum(before).astype(jnp.int32), step)
    stop = jnp.minimum(jnp.sum(until).astype(jnp.int32), step + REACH)
    needed = stop - start
    own_column = jnp.broadcast_to(own, (BLK, BLK)).T[:, 0:1]
    scale = LOG2E / DH**0.5

    def window(size):
        begin = jnp.minimum(start, step + REACH - size)
        far = jnp.concatenate([labels[begin + t, 0:1, :] for t in range(size)], axis=1).astype(jnp.float32)
        match = own_column == far
        for head in range(PAIR // DH):
            lanes = slice(head * DH, (head + 1) * DH)
            query = query_ref[0, :, lanes]
            key = keys[pl.ds(begin, size), :, lanes].reshape(size * BLK, DH)
            value = values[pl.ds(begin, size), :, lanes].reshape(size * BLK, DH)
            scores = lax.dot_general(query, key, (((1,), (1,)), ((), ())), preferred_element_type=jnp.float32)
            scores = jnp.where(match, scores, -1e30)
            peak = jnp.max(scores, axis=1, keepdims=True)
            expo = jnp.exp2((scores - peak) * scale)
            total = jnp.sum(expo, axis=1, keepdims=True)
            summed = jnp.dot(expo.astype(jnp.bfloat16), value, preferred_element_type=jnp.float32)
            out_ref[0, 0, :, lanes] = (summed / total).astype(jnp.bfloat16)

    smaller = 0
    for size in WINDOWS:
        pl.when((needed > smaller) & (needed <= size))(functools.partial(window, size))
        smaller = size


def attention(here, query, kv):
    return pl.pallas_call(
        attention_body,
        grid_spec=pltpu.PrefetchScalarGridSpec(
            num_scalar_prefetch=1,
            grid=(LINE,),
            in_specs=[pl.BlockSpec((1, BLK, PAIR), lambda i, here: (i, 0, 0))] + [ANY] * 3,
            out_specs=pl.BlockSpec((1, 1, BLK, PAIR), lambda i, here: ((i // 2) ^ here[0], i % 2, 0, 0)),
            scratch_shapes=[
                pltpu.VMEM((BLOCKS, BLK, PAIR), jnp.bfloat16),
                pltpu.VMEM((BLOCKS, BLK, PAIR), jnp.bfloat16),
                pltpu.VMEM((BLOCKS, MARK, PAIR), jnp.bfloat16),
                pltpu.SemaphoreType.DMA((9,)),
            ],
        ),
        out_shape=jax.ShapeDtypeStruct((CHIPS, 2, BLK, PAIR), jnp.bfloat16),
        compiler_params=pltpu.CompilerParams(dimension_semantics=("arbitrary",), vmem_limit_bytes=24 * MIB),
        cost_estimate=pl.CostEstimate(flops=2400000000, bytes_accessed=9 * MIB, transcendentals=4700000),
        name="attention",
    )(here, query, *kv)


def project_body(place_ref, own_ref, got_ref, hidden_ref, matrix_ref, out_ref, rows_ref, total_ref, sems):
    copies = []
    for n in range(LINE):
        first = pl.multiple_of(place_ref[1 + n] * PAIR, PAIR)
        copies.append(pltpu.make_async_copy(matrix_ref.at[pl.ds(first, PAIR)], rows_ref.at[n], sems.at[n]))
    for copy in copies:
        copy.start()
    total_ref[...] = hidden_ref[...].astype(jnp.float32)
    columns = out_ref.shape[1]
    for first in range(0, LINE, 2):
        for n in (first, first + 1):
            copies[n].wait()
        rows = [own_ref[n] if n < CHIPS else got_ref[n - CHIPS] for n in (first, first + 1)]
        for at in range(0, columns, PAIR):
            lanes = slice(at, at + PAIR)
            product = jnp.dot(rows[0], rows_ref[first, :, lanes], preferred_element_type=jnp.float32)
            product += jnp.dot(rows[1], rows_ref[first + 1, :, lanes], preferred_element_type=jnp.float32)
            if first < LINE - 2:
                total_ref[:, lanes] += product
            else:
                out_ref[:, lanes] = (total_ref[:, lanes] + product).astype(jnp.bfloat16)


def project(place, attended, hidden, matrix):
    columns = matrix.shape[1]
    rows = pl.BlockSpec((CHIPS, BLK, PAIR), lambda i, place: (0, 0, 0))
    return pl.pallas_call(
        project_body,
        grid_spec=pltpu.PrefetchScalarGridSpec(
            num_scalar_prefetch=1,
            grid=(1,),
            in_specs=[rows, rows, pl.BlockSpec((BLK, columns), lambda i, place: (0, place[0])), ANY],
            out_specs=pl.BlockSpec((BLK, columns), lambda i, place: (0, 0)),
            scratch_shapes=[
                pltpu.VMEM((LINE, PAIR, columns), jnp.bfloat16),
                pltpu.VMEM((BLK, columns), jnp.float32),
                pltpu.SemaphoreType.DMA((LINE,)),
            ],
        ),
        out_shape=jax.ShapeDtypeStruct((BLK, columns), jnp.bfloat16),
        compiler_params=pltpu.CompilerParams(dimension_semantics=("arbitrary",), vmem_limit_bytes=60 * MIB),
        cost_estimate=pl.CostEstimate(flops=0, bytes_accessed=0, transcendentals=0),
        name="project",
    )(place, *attended, hidden, matrix)


def after(value, *others):
    return lax.optimization_barrier((value, *others))[0]


def to_next_section(value):
    return lax.ppermute(value, ("x", "zh"), [(s, (s + 1) % 8) for s in range(8)])


def to_other_core(value):
    return lax.ppermute(value, "c", [(0, 1), (1, 0)])


def across(pieces):
    return [lax.ppermute(piece, "zl", [(z, z ^ (k + 1)) for z in range(CHIPS)]) for k, piece in enumerate(pieces)]


def on_device(hidden, query, keyv, value, segments, out_weight):
    core, chip = lax.axis_index("c"), lax.axis_index("zl")
    here = jnp.stack([chip, core]).astype(jnp.int32)
    hidden, weight = hidden[0], out_weight[0]
    half = hidden.shape[1] // 2
    part = half // PARTS

    near = lax.all_gather(weight, ("zl", "c"), axis=0, tiled=True)

    kv, kv_other = pack(here, keyv[0], value[0], segments)
    kv_got = to_other_core(kv_other)
    heads, heads_other = pack(here, query[0])
    heads_got = to_other_core(heads_other)
    kv_far = across(combine(kv, kv_got))
    heads_out = combine(heads, heads_got)
    kv_far = [after(piece, *heads_out) for piece in kv_far]
    heads_far = across(heads_out)
    kv = assemble(here, kv, kv_got, kv_far)
    left = lax.ppermute(kv[LINE - SPAN :], "y", [(i, i + 1) for i in range(3)])
    right = lax.ppermute(kv[:SPAN], "y", [(i + 1, i) for i in range(3)])
    heads = assemble(here, heads, heads_got, heads_far)

    near = after(near, left, right, *heads_far)
    mine = []
    for p in range(PARTS):
        piece = lax.dynamic_slice_in_dim(near, core * half + p * part, part, 1)
        mine.append(lax.all_gather(piece, "y", axis=0, tiled=True))

    attended = attention(here, heads, (left, kv, right))
    far = across([attended[k] for k in range(1, CHIPS)])
    own, send = divide(here, attended, far)
    attended = [own, to_other_core(send)]

    out = jnp.zeros(hidden.shape, hidden.dtype)
    chips = chip ^ jnp.arange(CHIPS, dtype=jnp.int32)
    order = jnp.concatenate([2 * chips + core, 2 * chips + 1 - core])
    made, arrived = [], []
    for p in range(PARTS):
        matrix = after(mine[p], *attended, *made, *arrived)
        for which, matrix in ((core, matrix), (1 - core, to_other_core(matrix))):
            place = jnp.concatenate([(which * PARTS + p)[None], order]).astype(jnp.int32)
            ready = [after(rows, *made[-1:], *arrived[: 2 * p]) for rows in attended]
            made.append(project(place, ready, hidden, matrix))
            arrived.append(to_next_section(made[-1]))
            out = lax.dynamic_update_slice(out, arrived[-1], (0, which * half + p * part))
    return out[None]


def solution(mesh):
    wide = Mesh(mesh.devices.reshape(4, 2, 4, 4, 2), ("x", "zh", "y", "zl", "c"))
    section, ctx = ("x", "zh"), ("y", "zl", "c")
    return jax.shard_map(
        on_device,
        mesh=wide,
        in_specs=(
            P(section, ctx, None),
            P(section, ctx, None),
            P(section, ctx, None),
            P(section, ctx, None),
            P(section, ctx),
            P(section, ctx, None),
        ),
        out_specs=P(section, ctx, None),
        check_vma=False,
    )
```

```python
import functools

import jax
import jax.numpy as jnp
from jax import lax
from jax.experimental import pallas as pl
from jax.experimental.pallas import tpu as pltpu
from jax.sharding import Mesh, PartitionSpec as P

DH = 128
SPAN = 3
BLK = 256
LINE = 8
PAIR = 256
REACH = 2 * SPAN + 1
BLOCKS = LINE + 2 * SPAN
MARK = 16
LOG2E = 1.4426950408889634
WINDOWS = (2, 3, 4, 5, 7)
PARTS = 2
CHIPS = LINE // 2
MIB = 1024 * 1024


ANY = pl.BlockSpec(memory_space=pl.ANY)
WHOLE = pl.BlockSpec(memory_space=pltpu.VMEM)
SCALARS = pl.BlockSpec(memory_space=pltpu.SMEM)


def run_copies(pairs, sems):
    copies = [pltpu.make_async_copy(src, dst, sems.at[index]) for index, (src, dst) in enumerate(pairs)]
    for copy in copies:
        copy.start()
    for copy in copies:
        copy.wait()


def pack_body(here_ref, *refs):
    arrays, mine_ref, other_ref = refs[:-2], refs[-2], refs[-1]
    chip, core = here_ref[0], here_ref[1]
    for j in range(LINE):

        def store(out_ref, j=j):
            for index, ref in enumerate(arrays):
                if ref.shape[0] == BLK:
                    piece = ref[:, j * PAIR : (j + 1) * PAIR]
                    out_ref[(j // 2) ^ chip, index * BLK : (index + 1) * BLK] = piece
                else:
                    labels = (ref[...] + 1).astype(jnp.float32)
                    out_ref[(j // 2) ^ chip, index * BLK :] = jnp.broadcast_to(labels, (MARK, BLK)).astype(jnp.bfloat16)

        pl.when(core == j % 2)(functools.partial(store, mine_ref))
        pl.when(core != j % 2)(functools.partial(store, other_ref))


def pack(here, *arrays):
    height = sum(BLK if array.shape[0] == BLK else MARK for array in arrays)
    out = jax.ShapeDtypeStruct((CHIPS, height, PAIR), jnp.bfloat16)
    return pl.pallas_call(
        pack_body,
        in_specs=[SCALARS] + [WHOLE] * len(arrays),
        out_specs=[WHOLE, WHOLE],
        out_shape=[out, out],
        compiler_params=pltpu.CompilerParams(vmem_limit_bytes=16 * MIB),
        cost_estimate=pl.CostEstimate(flops=0, bytes_accessed=2 * MIB, transcendentals=0),
        name="pack",
    )(here, *arrays)


def combine_body(mine_ref, got_ref, *refs):
    outs, sems = refs[:-1], refs[-1]
    run_copies([(ref.at[k], out.at[s]) for k, out in enumerate(outs) for s, ref in enumerate((mine_ref, got_ref))], sems)


def combine(mine, got):
    out = jax.ShapeDtypeStruct((2, *mine.shape[1:]), jnp.bfloat16)
    return pl.pallas_call(
        combine_body,
        in_specs=[ANY] * 2,
        out_specs=[pl.BlockSpec(memory_space=pltpu.HBM)] * CHIPS,
        out_shape=[out] * CHIPS,
        scratch_shapes=[pltpu.SemaphoreType.DMA((LINE,))],
        compiler_params=pltpu.CompilerParams(vmem_limit_bytes=4 * MIB),
        cost_estimate=pl.CostEstimate(flops=0, bytes_accessed=2 * MIB, transcendentals=0),
        name="combine",
    )(mine, got)


def assemble_body(here_ref, *refs):
    far, out_ref, sems = refs[:-2], refs[-2], refs[-1]
    chip, core = here_ref[0], here_ref[1]
    pairs = []
    for k, ref in enumerate(far):
        place = 2 * (chip ^ k)
        pairs += [(ref.at[0], out_ref.at[place + core]), (ref.at[1], out_ref.at[place + 1 - core])]
    run_copies(pairs, sems)


def assemble(here, far):
    return pl.pallas_call(
        assemble_body,
        in_specs=[SCALARS] + [ANY] * CHIPS,
        out_specs=ANY,
        out_shape=jax.ShapeDtypeStruct((LINE, *far[0].shape[1:]), jnp.bfloat16),
        scratch_shapes=[pltpu.SemaphoreType.DMA((LINE,))],
        compiler_params=pltpu.CompilerParams(vmem_limit_bytes=4 * MIB),
        cost_estimate=pl.CostEstimate(flops=0, bytes_accessed=2 * MIB, transcendentals=0),
        name="assemble",
    )(here, *far)


def divide_body(here_ref, near_ref, *refs):
    far, own_ref, send_ref, sems = refs[:-3], refs[-3], refs[-2], refs[-1]
    core = here_ref[1]
    pairs = []
    for k, ref in enumerate((near_ref.at[0], *far)):
        pairs += [(ref.at[core], own_ref.at[k]), (ref.at[1 - core], send_ref.at[k])]
    run_copies(pairs, sems)


def divide(here, near, far):
    out = jax.ShapeDtypeStruct((CHIPS, BLK, PAIR), jnp.bfloat16)
    return pl.pallas_call(
        divide_body,
        in_specs=[SCALARS] + [ANY] * CHIPS,
        out_specs=[ANY, ANY],
        out_shape=[out, out],
        scratch_shapes=[pltpu.SemaphoreType.DMA((LINE,))],
        compiler_params=pltpu.CompilerParams(vmem_limit_bytes=4 * MIB),
        cost_estimate=pl.CostEstimate(flops=0, bytes_accessed=2 * MIB, transcendentals=0),
        name="divide",
    )(here, near, *far)


def attention_body(here_ref, query_ref, left_ref, kv_ref, right_ref, out_ref, keys, values, labels, sems):
    step = pl.program_id(0)

    @pl.when(step == 0)
    def _():
        pairs = []
        for dst, first, rows in ((keys, 0, BLK), (values, BLK, BLK), (labels, 2 * BLK, MARK)):
            at = 0
            for src, count in ((left_ref, SPAN), (kv_ref, LINE), (right_ref, SPAN)):
                pairs.append((src.at[:, pl.ds(first, rows)], dst.at[pl.ds(at, count)]))
                at += count
        run_copies(pairs, sems)

    own = jnp.max(labels[step + SPAN].astype(jnp.float32), axis=0, keepdims=True)
    first, last = jnp.min(own), jnp.max(own)
    marks = jnp.max(labels[...].astype(jnp.float32), axis=1)
    top, low = jnp.max(marks, axis=1, keepdims=True), jnp.min(marks, axis=1, keepdims=True)
    place = lax.broadcasted_iota(jnp.int32, (BLOCKS, 1), 0)
    beyond = (place >= SPAN + LINE) & (top == 0.0)
    before = jnp.where((top < first) & ~beyond, 1.0, 0.0)
    until = jnp.where((low <= last) & ~beyond, 1.0, 0.0)
    start = jnp.maximum(jnp.sum(before).astype(jnp.int32), step)
    stop = jnp.minimum(jnp.sum(until).astype(jnp.int32), step + REACH)
    needed = stop - start
    own_column = jnp.broadcast_to(own, (BLK, BLK)).T[:, 0:1]
    scale = LOG2E / DH**0.5

    def window(size):
        begin = jnp.minimum(start, step + REACH - size)
        far = jnp.concatenate([labels[begin + t, 0:1, :] for t in range(size)], axis=1).astype(jnp.float32)
        match = own_column == far
        for head in range(PAIR // DH):
            lanes = slice(head * DH, (head + 1) * DH)
            query = query_ref[0, :, lanes]
            key = keys[pl.ds(begin, size), :, lanes].reshape(size * BLK, DH)
            value = values[pl.ds(begin, size), :, lanes].reshape(size * BLK, DH)
            scores = lax.dot_general(query, key, (((1,), (1,)), ((), ())), preferred_element_type=jnp.float32)
            scores = jnp.where(match, scores, -1e30)
            peak = jnp.max(scores, axis=1, keepdims=True)
            expo = jnp.exp2((scores - peak) * scale)
            total = jnp.sum(expo, axis=1, keepdims=True)
            summed = jnp.dot(expo.astype(jnp.bfloat16), value, preferred_element_type=jnp.float32)
            out_ref[0, 0, :, lanes] = (summed / total).astype(jnp.bfloat16)

    smaller = 0
    for size in WINDOWS:
        pl.when((needed > smaller) & (needed <= size))(functools.partial(window, size))
        smaller = size


def attention(here, query, kv):
    return pl.pallas_call(
        attention_body,
        grid_spec=pltpu.PrefetchScalarGridSpec(
            num_scalar_prefetch=1,
            grid=(LINE,),
            in_specs=[pl.BlockSpec((1, BLK, PAIR), lambda i, here: (i, 0, 0))] + [ANY] * 3,
            out_specs=pl.BlockSpec((1, 1, BLK, PAIR), lambda i, here: ((i // 2) ^ here[0], i % 2, 0, 0)),
            scratch_shapes=[
                pltpu.VMEM((BLOCKS, BLK, PAIR), jnp.bfloat16),
                pltpu.VMEM((BLOCKS, BLK, PAIR), jnp.bfloat16),
                pltpu.VMEM((BLOCKS, MARK, PAIR), jnp.bfloat16),
                pltpu.SemaphoreType.DMA((9,)),
            ],
        ),
        out_shape=jax.ShapeDtypeStruct((CHIPS, 2, BLK, PAIR), jnp.bfloat16),
        compiler_params=pltpu.CompilerParams(dimension_semantics=("arbitrary",), vmem_limit_bytes=24 * MIB),
        cost_estimate=pl.CostEstimate(flops=2400000000, bytes_accessed=9 * MIB, transcendentals=4700000),
        name="attention",
    )(here, query, *kv)


def project_body(place_ref, own_ref, got_ref, hidden_ref, matrix_ref, out_ref, rows_ref, rest_ref, total_ref, sems):
    columns = out_ref.shape[1]
    copies = []
    for n in range(LINE):
        first = pl.multiple_of(place_ref[1 + n] * PAIR, PAIR)
        copies.append(pltpu.make_async_copy(matrix_ref.at[pl.ds(first, PAIR)], rows_ref.at[n], sems.at[n]))
    first = pl.multiple_of(place_ref[0] * columns, columns)
    rest = pltpu.make_async_copy(hidden_ref.at[:, pl.ds(first, columns)], rest_ref, sems.at[LINE])
    for copy in (*copies, rest):
        copy.start()
    for first in range(0, LINE, 2):
        for n in (first, first + 1):
            copies[n].wait()
        if first == LINE - 2:
            rest.wait()
        rows = [own_ref[n] if n < CHIPS else got_ref[n - CHIPS] for n in (first, first + 1)]
        for at in range(0, columns, PAIR):
            lanes = slice(at, at + PAIR)
            product = jnp.dot(rows[0], rows_ref[first, :, lanes], preferred_element_type=jnp.float32)
            product += jnp.dot(rows[1], rows_ref[first + 1, :, lanes], preferred_element_type=jnp.float32)
            if first == 0:
                total_ref[:, lanes] = product
            elif first < LINE - 2:
                total_ref[:, lanes] += product
            else:
                total = rest_ref[:, lanes].astype(jnp.float32) + (total_ref[:, lanes] + product)
                out_ref[:, lanes] = total.astype(jnp.bfloat16)


def project(place, attended, hidden, matrix):
    columns = matrix.shape[1]
    return pl.pallas_call(
        project_body,
        in_specs=[SCALARS, WHOLE, WHOLE, ANY, ANY],
        out_specs=WHOLE,
        scratch_shapes=[
            pltpu.VMEM((LINE, PAIR, columns), jnp.bfloat16),
            pltpu.VMEM((BLK, columns), jnp.bfloat16),
            pltpu.VMEM((BLK, columns), jnp.float32),
            pltpu.SemaphoreType.DMA((LINE + 1,)),
        ],
        out_shape=jax.ShapeDtypeStruct((BLK, columns), jnp.bfloat16),
        compiler_params=pltpu.CompilerParams(vmem_limit_bytes=60 * MIB),
        cost_estimate=pl.CostEstimate(flops=2, bytes_accessed=2, transcendentals=0),
        name="project",
    )(place, *attended, hidden, matrix)


def after(value, *others):
    return lax.optimization_barrier((value, *others))[0]


def to_next_section(value):
    return lax.ppermute(value, ("x", "zh"), [(s, (s + 1) % 8) for s in range(8)])


def to_other_core(value):
    return lax.ppermute(value, "c", [(0, 1), (1, 0)])


def across(pieces):
    far = [lax.ppermute(piece, "zl", [(z, z ^ k) for z in range(CHIPS)]) for k, piece in enumerate(pieces) if k]
    return [pieces[0], *far]


def on_device(hidden, query, keyv, value, segments, out_weight):
    core, chip = lax.axis_index("c"), lax.axis_index("zl")
    here = jnp.stack([chip, core]).astype(jnp.int32)
    hidden, weight = hidden[0], out_weight[0]
    half = hidden.shape[1] // 2
    part = half // PARTS

    kv, kv_other = pack(here, keyv[0], value[0], segments)
    kv_out = combine(kv, to_other_core(kv_other))
    heads, heads_other = pack(here, query[0])
    heads_out = combine(heads, to_other_core(heads_other))

    rows = [lax.dynamic_slice_in_dim(weight, which * half, half, 1) for which in (core, 1 - core)]
    rows[1] = to_other_core(rows[1])
    rows = [jnp.where(core == place, *rows) for place in (0, 1)]
    rows = [jnp.concatenate([row[:, p * part : (p + 1) * part] for row in rows], axis=0) for p in range(PARTS)]

    def gather(piece, axis):
        return lax.all_gather(piece, axis, axis=0, tiled=True)

    first = gather(rows[0], "zl")
    kv_far = across(kv_out)
    first = after(first, kv_far[1], kv_far[3], *heads_out)
    kv_far[2] = after(kv_far[2], first)
    first = gather(first, "y")
    heads_far = across(heads_out)
    kv = assemble(here, kv_far)
    left = lax.ppermute(kv[LINE - SPAN :], "y", [(i, i + 1) for i in range(3)])
    right = lax.ppermute(kv[:SPAN], "y", [(i + 1, i) for i in range(3)])
    heads = assemble(here, heads_far)
    second = gather(after(rows[1], left, right, *heads_far, first), "zl")

    attended = attention(here, heads, (left, kv, right))
    far = across([attended[k] for k in range(CHIPS)])
    first = after(first, *far)
    own, send = divide(here, attended, far[1:])
    attended = [own, to_other_core(send)]
    second = gather(after(second, *attended), "y")

    out = jnp.zeros(hidden.shape, hidden.dtype)
    chips = chip ^ jnp.arange(CHIPS, dtype=jnp.int32)
    order = jnp.concatenate([2 * chips + core, 2 * chips + 1 - core])
    made, arrived = [], []
    for p, matrix in enumerate((first, after(second, *attended))):
        matrix = after(matrix, *made, *arrived)
        for which, matrix in ((core, matrix), (1 - core, to_other_core(matrix))):
            place = jnp.concatenate([(which * PARTS + p)[None], order]).astype(jnp.int32)
            ready = [after(rows, *made[-1:], *arrived[: 2 * p]) for rows in attended]
            made.append(project(place, ready, hidden, matrix))
            arrived.append(to_next_section(made[-1]))
            out = lax.dynamic_update_slice(out, arrived[-1], (0, which * half + p * part))
    return out[None]


def solution(mesh):
    wide = Mesh(mesh.devices.reshape(4, 2, 4, 4, 2), ("x", "zh", "y", "zl", "c"))
    section, ctx = ("x", "zh"), ("y", "zl", "c")
    return jax.shard_map(
        on_device,
        mesh=wide,
        in_specs=(
            P(section, ctx, None),
            P(section, ctx, None),
            P(section, ctx, None),
            P(section, ctx, None),
            P(section, ctx),
            P(section, ctx, None),
        ),
        out_specs=P(section, ctx, None),
        check_vma=False,
    )
```

```python
import functools

import jax
import jax.numpy as jnp
from jax import lax
from jax.experimental import pallas as pl
from jax.experimental.pallas import tpu as pltpu
from jax.sharding import Mesh, PartitionSpec as P

DH = 128
SPAN = 3
BLK = 256
LINE = 8
PAIR = 256
REACH = 2 * SPAN + 1
BLOCKS = LINE + 2 * SPAN
MARK = 16
LOG2E = 1.4426950408889634
WINDOWS = (2, 3, 4, 5, 7)
PARTS = 2
CHIPS = LINE // 2
MIB = 1024 * 1024


ANY = pl.BlockSpec(memory_space=pl.ANY)
WHOLE = pl.BlockSpec(memory_space=pltpu.VMEM)
SCALARS = pl.BlockSpec(memory_space=pltpu.SMEM)


def run_copies(pairs, sems):
    copies = [pltpu.make_async_copy(src, dst, sems.at[index]) for index, (src, dst) in enumerate(pairs)]
    for copy in copies:
        copy.start()
    for copy in copies:
        copy.wait()


def pack_body(here_ref, *refs):
    arrays, mine_ref, other_ref = refs[:-2], refs[-2], refs[-1]
    chip, core = here_ref[0], here_ref[1]
    for j in range(LINE):

        def store(out_ref, j=j):
            for index, ref in enumerate(arrays):
                if ref.shape[0] == BLK:
                    piece = ref[:, j * PAIR : (j + 1) * PAIR]
                    out_ref[(j // 2) ^ chip, index * BLK : (index + 1) * BLK] = piece
                else:
                    labels = (ref[...] + 1).astype(jnp.float32)
                    out_ref[(j // 2) ^ chip, index * BLK :] = jnp.broadcast_to(labels, (MARK, BLK)).astype(jnp.bfloat16)

        pl.when(core == j % 2)(functools.partial(store, mine_ref))
        pl.when(core != j % 2)(functools.partial(store, other_ref))


def pack(here, *arrays):
    height = sum(BLK if array.shape[0] == BLK else MARK for array in arrays)
    out = jax.ShapeDtypeStruct((CHIPS, height, PAIR), jnp.bfloat16)
    return pl.pallas_call(
        pack_body,
        in_specs=[SCALARS] + [WHOLE] * len(arrays),
        out_specs=[WHOLE, WHOLE],
        out_shape=[out, out],
        compiler_params=pltpu.CompilerParams(vmem_limit_bytes=16 * MIB),
        cost_estimate=pl.CostEstimate(flops=0, bytes_accessed=2 * MIB, transcendentals=0),
        name="pack",
    )(here, *arrays)


def combine_body(mine_ref, got_ref, *refs):
    outs, sems = refs[:-1], refs[-1]
    run_copies([(ref.at[k], out.at[s]) for k, out in enumerate(outs) for s, ref in enumerate((mine_ref, got_ref))], sems)


def combine(mine, got):
    out = jax.ShapeDtypeStruct((2, *mine.shape[1:]), jnp.bfloat16)
    return pl.pallas_call(
        combine_body,
        in_specs=[ANY] * 2,
        out_specs=[pl.BlockSpec(memory_space=pltpu.HBM)] * CHIPS,
        out_shape=[out] * CHIPS,
        scratch_shapes=[pltpu.SemaphoreType.DMA((LINE,))],
        compiler_params=pltpu.CompilerParams(vmem_limit_bytes=4 * MIB),
        cost_estimate=pl.CostEstimate(flops=0, bytes_accessed=2 * MIB, transcendentals=0),
        name="combine",
    )(mine, got)


def assemble_body(here_ref, *refs):
    far, out_ref, sems = refs[:-2], refs[-2], refs[-1]
    chip, core = here_ref[0], here_ref[1]
    pairs = []
    for k, ref in enumerate(far):
        place = 2 * (chip ^ k)
        pairs += [(ref.at[0], out_ref.at[place + core]), (ref.at[1], out_ref.at[place + 1 - core])]
    run_copies(pairs, sems)


def assemble(here, far):
    return pl.pallas_call(
        assemble_body,
        in_specs=[SCALARS] + [ANY] * CHIPS,
        out_specs=ANY,
        out_shape=jax.ShapeDtypeStruct((LINE, *far[0].shape[1:]), jnp.bfloat16),
        scratch_shapes=[pltpu.SemaphoreType.DMA((LINE,))],
        compiler_params=pltpu.CompilerParams(vmem_limit_bytes=4 * MIB),
        cost_estimate=pl.CostEstimate(flops=0, bytes_accessed=2 * MIB, transcendentals=0),
        name="assemble",
    )(here, *far)


def divide_body(here_ref, near_ref, *refs):
    far, own_ref, send_ref, sems = refs[:-3], refs[-3], refs[-2], refs[-1]
    core = here_ref[1]
    pairs = []
    for k, ref in enumerate((near_ref.at[0], *far)):
        pairs += [(ref.at[core], own_ref.at[k]), (ref.at[1 - core], send_ref.at[k])]
    run_copies(pairs, sems)


def divide(here, near, far):
    out = jax.ShapeDtypeStruct((CHIPS, BLK, PAIR), jnp.bfloat16)
    return pl.pallas_call(
        divide_body,
        in_specs=[SCALARS] + [ANY] * CHIPS,
        out_specs=[ANY, ANY],
        out_shape=[out, out],
        scratch_shapes=[pltpu.SemaphoreType.DMA((LINE,))],
        compiler_params=pltpu.CompilerParams(vmem_limit_bytes=4 * MIB),
        cost_estimate=pl.CostEstimate(flops=0, bytes_accessed=2 * MIB, transcendentals=0),
        name="divide",
    )(here, near, *far)


def attention_body(here_ref, query_ref, left_ref, kv_ref, right_ref, out_ref, keys, values, labels, bounds, sems):
    step = pl.program_id(0)

    @pl.when(step == 0)
    def _():
        pairs = []
        for dst, first, rows in ((keys, 0, BLK), (values, BLK, BLK), (labels, 2 * BLK, MARK)):
            at = 0
            for src, count in ((left_ref, SPAN), (kv_ref, LINE), (right_ref, SPAN)):
                pairs.append((src.at[:, pl.ds(first, rows)], dst.at[pl.ds(at, count)]))
                at += count
        run_copies(pairs, sems)

        marks = jnp.max(labels[...].astype(jnp.float32), axis=1)
        top, low = jnp.max(marks, axis=1, keepdims=True), jnp.min(marks, axis=1, keepdims=True)
        place = lax.broadcasted_iota(jnp.int32, (BLOCKS, 1), 0)
        beyond = (place >= SPAN + LINE) & (top == 0.0)
        for index, value in enumerate((top, low)):
            bounds[index] = jnp.broadcast_to(jnp.where(beyond, 99.0, value), (BLOCKS, DH))

    own = jnp.max(labels[step + SPAN].astype(jnp.float32), axis=0, keepdims=True)
    before = bounds[0] < jnp.min(own, axis=1, keepdims=True)
    until = bounds[1] <= jnp.max(own, axis=1, keepdims=True)
    counts = jnp.sum(jnp.where(before, 16.0, 0.0) + jnp.where(until, 1.0, 0.0), axis=0, keepdims=True)
    both = jnp.max(counts).astype(jnp.int32)
    start, stop = jnp.maximum(both // 16, step), jnp.minimum(both % 16, step + REACH)
    needed = stop - start
    own_column = jnp.broadcast_to(own, (BLK, BLK)).T[:, 0:1]
    scale = LOG2E / DH**0.5

    def window(size):
        begin = jnp.minimum(start, step + REACH - size)
        far = jnp.concatenate([labels[begin + t, 0:1, :] for t in range(size)], axis=1).astype(jnp.float32)
        match = own_column == far
        for head in range(PAIR // DH):
            lanes = slice(head * DH, (head + 1) * DH)
            query = query_ref[0, :, lanes]
            key = keys[pl.ds(begin, size), :, lanes].reshape(size * BLK, DH)
            value = values[pl.ds(begin, size), :, lanes].reshape(size * BLK, DH)
            scores = lax.dot_general(query, key, (((1,), (1,)), ((), ())), preferred_element_type=jnp.float32)
            scores = jnp.where(match, scores, -1e30)
            peak = jnp.max(scores, axis=1, keepdims=True)
            expo = jnp.exp2((scores - peak) * scale)
            total = jnp.sum(expo, axis=1, keepdims=True)
            summed = jnp.dot(expo.astype(jnp.bfloat16), value, preferred_element_type=jnp.float32)
            out_ref[0, 0, :, lanes] = (summed / total).astype(jnp.bfloat16)

    smaller = 0
    for size in WINDOWS:
        pl.when((needed > smaller) & (needed <= size))(functools.partial(window, size))
        smaller = size


def attention(here, query, kv):
    return pl.pallas_call(
        attention_body,
        grid_spec=pltpu.PrefetchScalarGridSpec(
            num_scalar_prefetch=1,
            grid=(LINE,),
            in_specs=[pl.BlockSpec((1, BLK, PAIR), lambda i, here: (i, 0, 0))] + [ANY] * 3,
            out_specs=pl.BlockSpec((1, 1, BLK, PAIR), lambda i, here: ((i // 2) ^ here[0], i % 2, 0, 0)),
            scratch_shapes=[
                pltpu.VMEM((BLOCKS, BLK, PAIR), jnp.bfloat16),
                pltpu.VMEM((BLOCKS, BLK, PAIR), jnp.bfloat16),
                pltpu.VMEM((BLOCKS, MARK, PAIR), jnp.bfloat16),
                pltpu.VMEM((2, BLOCKS, DH), jnp.float32),
                pltpu.SemaphoreType.DMA((9,)),
            ],
        ),
        out_shape=jax.ShapeDtypeStruct((CHIPS, 2, BLK, PAIR), jnp.bfloat16),
        compiler_params=pltpu.CompilerParams(dimension_semantics=("arbitrary",), vmem_limit_bytes=24 * MIB),
        cost_estimate=pl.CostEstimate(flops=2400000000, bytes_accessed=9 * MIB, transcendentals=4700000),
        name="attention",
    )(here, query, *kv)


def project_body(place_ref, own_ref, got_ref, hidden_ref, matrix_ref, out_ref, rows_ref, rest_ref, total_ref, sems):
    columns = out_ref.shape[1]
    copies = []
    for n in range(LINE):
        first = pl.multiple_of(place_ref[1 + n] * PAIR, PAIR)
        copies.append(pltpu.make_async_copy(matrix_ref.at[pl.ds(first, PAIR)], rows_ref.at[n], sems.at[n]))
    first = pl.multiple_of(place_ref[0] * columns, columns)
    rest = pltpu.make_async_copy(hidden_ref.at[:, pl.ds(first, columns)], rest_ref, sems.at[LINE])
    for copy in (*copies, rest):
        copy.start()
    for first in range(0, LINE, 2):
        for n in (first, first + 1):
            copies[n].wait()
        if first == LINE - 2:
            rest.wait()
        rows = [own_ref[n] if n < CHIPS else got_ref[n - CHIPS] for n in (first, first + 1)]
        for at in range(0, columns, PAIR):
            lanes = slice(at, at + PAIR)
            product = jnp.dot(rows[0], rows_ref[first, :, lanes], preferred_element_type=jnp.float32)
            product += jnp.dot(rows[1], rows_ref[first + 1, :, lanes], preferred_element_type=jnp.float32)
            if first == 0:
                total_ref[:, lanes] = product
            elif first < LINE - 2:
                total_ref[:, lanes] += product
            else:
                total = rest_ref[:, lanes].astype(jnp.float32) + (total_ref[:, lanes] + product)
                out_ref[:, lanes] = total.astype(jnp.bfloat16)


def project(place, attended, hidden, matrix):
    columns = matrix.shape[1]
    return pl.pallas_call(
        project_body,
        in_specs=[SCALARS, WHOLE, WHOLE, ANY, ANY],
        out_specs=WHOLE,
        scratch_shapes=[
            pltpu.VMEM((LINE, PAIR, columns), jnp.bfloat16),
            pltpu.VMEM((BLK, columns), jnp.bfloat16),
            pltpu.VMEM((BLK, columns), jnp.float32),
            pltpu.SemaphoreType.DMA((LINE + 1,)),
        ],
        out_shape=jax.ShapeDtypeStruct((BLK, columns), jnp.bfloat16),
        compiler_params=pltpu.CompilerParams(vmem_limit_bytes=60 * MIB),
        cost_estimate=pl.CostEstimate(flops=2, bytes_accessed=2, transcendentals=0),
        name="project",
    )(place, *attended, hidden, matrix)


def after(value, *others):
    return lax.optimization_barrier((value, *others))[0]


def to_next_section(value):
    return lax.ppermute(value, ("x", "zh"), [(s, (s + 1) % 8) for s in range(8)])


def to_other_core(value):
    return lax.ppermute(value, "c", [(0, 1), (1, 0)])


def across(pieces):
    far = [lax.ppermute(piece, "zl", [(z, z ^ k) for z in range(CHIPS)]) for k, piece in enumerate(pieces) if k]
    return [pieces[0], *far]


def on_device(hidden, query, keyv, value, segments, out_weight):
    core, chip = lax.axis_index("c"), lax.axis_index("zl")
    here = jnp.stack([chip, core]).astype(jnp.int32)
    hidden, weight = hidden[0], out_weight[0]
    half = hidden.shape[1] // 2
    part = half // PARTS

    kv, kv_other = pack(here, keyv[0], value[0], segments)
    kv_out = combine(kv, to_other_core(kv_other))
    heads, heads_other = pack(here, query[0])
    heads_out = combine(heads, to_other_core(heads_other))

    rows = [lax.dynamic_slice_in_dim(weight, which * half, half, 1) for which in (core, 1 - core)]
    rows[1] = to_other_core(rows[1])
    rows = [jnp.where(core == place, *rows) for place in (0, 1)]
    rows = [jnp.concatenate([row[:, p * part : (p + 1) * part] for row in rows], axis=0) for p in range(PARTS)]

    def gather(piece, axis):
        return lax.all_gather(piece, axis, axis=0, tiled=True)

    first, second = gather(rows[0], "zl"), gather(rows[1], "zl")
    kv_far = across(kv_out)
    kv_far[2] = after(kv_far[2], *heads_out)
    heads_far = across(heads_out)
    kv = assemble(here, kv_far)
    first = gather(after(first, kv), "y")
    left = lax.ppermute(kv[LINE - SPAN :], "y", [(i, i + 1) for i in range(3)])
    right = lax.ppermute(kv[:SPAN], "y", [(i + 1, i) for i in range(3)])
    heads = assemble(here, heads_far)
    second = gather(after(second, left, right, *heads_far), "y")

    attended = attention(here, heads, (left, kv, right))
    far = across([attended[k] for k in range(CHIPS)])
    first = after(first, *far)
    own, send = divide(here, attended, far[1:])
    attended = [own, to_other_core(send)]

    out = jnp.zeros(hidden.shape, hidden.dtype)
    chips = chip ^ jnp.arange(CHIPS, dtype=jnp.int32)
    order = jnp.concatenate([2 * chips + core, 2 * chips + 1 - core])
    made, arrived = [], []
    for p, matrix in enumerate((first, second)):
        matrix = after(matrix, *attended, *made[-1:], *arrived[-2:-1])
        for which, matrix in ((core, matrix), (1 - core, to_other_core(matrix))):
            place = jnp.concatenate([(which * PARTS + p)[None], order]).astype(jnp.int32)
            ready = [after(rows, *made[-1:], *arrived[-2:-1]) for rows in attended]
            made.append(project(place, ready, hidden, matrix))
            arrived.append(to_next_section(made[-1]))
            out = lax.dynamic_update_slice(out, arrived[-1], (0, which * half + p * part))
    return out[None]


def solution(mesh):
    wide = Mesh(mesh.devices.reshape(4, 2, 4, 4, 2), ("x", "zh", "y", "zl", "c"))
    section, ctx = ("x", "zh"), ("y", "zl", "c")
    return jax.shard_map(
        on_device,
        mesh=wide,
        in_specs=(
            P(section, ctx, None),
            P(section, ctx, None),
            P(section, ctx, None),
            P(section, ctx, None),
            P(section, ctx),
            P(section, ctx, None),
        ),
        out_specs=P(section, ctx, None),
        check_vma=False,
    )
```

```python
import functools

import jax
import jax.numpy as jnp
from jax import lax
from jax.experimental import pallas as pl
from jax.experimental.pallas import tpu as pltpu
from jax.sharding import Mesh, PartitionSpec as P

DH = 128
SPAN = 3
BLK = 256
LINE = 8
PAIR = 256
REACH = 2 * SPAN + 1
BLOCKS = LINE + 2 * SPAN
MARK = 16
LOG2E = 1.4426950408889634
WINDOWS = (2, 3, 4, 5, 7)
PARTS = 2
CHIPS = LINE // 2
MASKS = (0, 3, 2, 1)
MIB = 1024 * 1024


ANY = pl.BlockSpec(memory_space=pl.ANY)
WHOLE = pl.BlockSpec(memory_space=pltpu.VMEM)
SCALARS = pl.BlockSpec(memory_space=pltpu.SMEM)


def run_copies(pairs, sems):
    copies = [pltpu.make_async_copy(src, dst, sems.at[index]) for index, (src, dst) in enumerate(pairs)]
    for copy in copies:
        copy.start()
    for copy in copies:
        copy.wait()


def pack_body(here_ref, *refs):
    arrays, mine_ref, other_ref = refs[:-2], refs[-2], refs[-1]
    chip, core = here_ref[0], here_ref[1]
    for j in range(LINE):

        def store(out_ref, j=j):
            for index, ref in enumerate(arrays):
                if ref.shape[0] == BLK:
                    piece = ref[:, j * PAIR : (j + 1) * PAIR]
                    out_ref[(CHIPS - ((j // 2) ^ chip)) % CHIPS, index * BLK : (index + 1) * BLK] = piece
                else:
                    labels = (ref[...] + 1).astype(jnp.float32)
                    out_ref[(CHIPS - ((j // 2) ^ chip)) % CHIPS, index * BLK :] = jnp.broadcast_to(labels, (MARK, BLK)).astype(jnp.bfloat16)

        pl.when(core == j % 2)(functools.partial(store, mine_ref))
        pl.when(core != j % 2)(functools.partial(store, other_ref))


def pack(here, *arrays):
    height = sum(BLK if array.shape[0] == BLK else MARK for array in arrays)
    out = jax.ShapeDtypeStruct((CHIPS, height, PAIR), jnp.bfloat16)
    return pl.pallas_call(
        pack_body,
        in_specs=[SCALARS] + [WHOLE] * len(arrays),
        out_specs=[WHOLE, WHOLE],
        out_shape=[out, out],
        compiler_params=pltpu.CompilerParams(vmem_limit_bytes=16 * MIB),
        cost_estimate=pl.CostEstimate(flops=0, bytes_accessed=2 * MIB, transcendentals=0),
        name="pack",
    )(here, *arrays)


def combine_body(mine_ref, got_ref, *refs):
    outs, sems = refs[:-1], refs[-1]
    run_copies([(ref.at[k], out.at[s]) for k, out in enumerate(outs) for s, ref in enumerate((mine_ref, got_ref))], sems)


def combine(mine, got):
    out = jax.ShapeDtypeStruct((2, *mine.shape[1:]), jnp.bfloat16)
    return pl.pallas_call(
        combine_body,
        in_specs=[ANY] * 2,
        out_specs=[pl.BlockSpec(memory_space=pltpu.HBM)] * CHIPS,
        out_shape=[out] * CHIPS,
        scratch_shapes=[pltpu.SemaphoreType.DMA((LINE,))],
        compiler_params=pltpu.CompilerParams(vmem_limit_bytes=4 * MIB),
        cost_estimate=pl.CostEstimate(flops=0, bytes_accessed=2 * MIB, transcendentals=0),
        name="combine",
    )(mine, got)


def assemble_body(here_ref, *refs):
    far, out_ref, sems = refs[:-2], refs[-2], refs[-1]
    chip, core = here_ref[0], here_ref[1]
    pairs = []
    for k, ref in enumerate(far):
        place = 2 * (chip ^ MASKS[k])
        pairs += [(ref.at[0], out_ref.at[place + core]), (ref.at[1], out_ref.at[place + 1 - core])]
    run_copies(pairs, sems)


def assemble(here, far):
    return pl.pallas_call(
        assemble_body,
        in_specs=[SCALARS] + [ANY] * CHIPS,
        out_specs=ANY,
        out_shape=jax.ShapeDtypeStruct((LINE, *far[0].shape[1:]), jnp.bfloat16),
        scratch_shapes=[pltpu.SemaphoreType.DMA((LINE,))],
        compiler_params=pltpu.CompilerParams(vmem_limit_bytes=4 * MIB),
        cost_estimate=pl.CostEstimate(flops=0, bytes_accessed=2 * MIB, transcendentals=0),
        name="assemble",
    )(here, *far)


def divide_body(here_ref, near_ref, *refs):
    far, own_ref, send_ref, sems = refs[:-3], refs[-3], refs[-2], refs[-1]
    core = here_ref[1]
    pairs = []
    for k, ref in enumerate((near_ref.at[0], *far)):
        pairs += [(ref.at[core], own_ref.at[k]), (ref.at[1 - core], send_ref.at[k])]
    run_copies(pairs, sems)


def divide(here, near, far):
    out = jax.ShapeDtypeStruct((CHIPS, BLK, PAIR), jnp.bfloat16)
    return pl.pallas_call(
        divide_body,
        in_specs=[SCALARS] + [ANY] * CHIPS,
        out_specs=[ANY, ANY],
        out_shape=[out, out],
        scratch_shapes=[pltpu.SemaphoreType.DMA((LINE,))],
        compiler_params=pltpu.CompilerParams(vmem_limit_bytes=4 * MIB),
        cost_estimate=pl.CostEstimate(flops=0, bytes_accessed=2 * MIB, transcendentals=0),
        name="divide",
    )(here, near, *far)


def attention_body(here_ref, query_ref, left_ref, kv_ref, right_ref, out_ref, keys, values, labels, bounds, sems):
    step = pl.program_id(0)

    @pl.when(step == 0)
    def _():
        pairs = []
        for dst, first, rows in ((keys, 0, BLK), (values, BLK, BLK), (labels, 2 * BLK, MARK)):
            at = 0
            for src, count in ((left_ref, SPAN), (kv_ref, LINE), (right_ref, SPAN)):
                pairs.append((src.at[:, pl.ds(first, rows)], dst.at[pl.ds(at, count)]))
                at += count
        run_copies(pairs, sems)

        marks = jnp.max(labels[...].astype(jnp.float32), axis=1)
        top, low = jnp.max(marks, axis=1, keepdims=True), jnp.min(marks, axis=1, keepdims=True)
        place = lax.broadcasted_iota(jnp.int32, (BLOCKS, 1), 0)
        beyond = (place >= SPAN + LINE) & (top == 0.0)
        for index, value in enumerate((top, low)):
            bounds[index] = jnp.broadcast_to(jnp.where(beyond, 99.0, value), (BLOCKS, DH))

    own = jnp.max(labels[step + SPAN].astype(jnp.float32), axis=0, keepdims=True)
    before = bounds[0] < jnp.min(own, axis=1, keepdims=True)
    until = bounds[1] <= jnp.max(own, axis=1, keepdims=True)
    counts = jnp.sum(jnp.where(before, 16.0, 0.0) + jnp.where(until, 1.0, 0.0), axis=0, keepdims=True)
    both = jnp.max(counts).astype(jnp.int32)
    start, stop = jnp.maximum(both // 16, step), jnp.minimum(both % 16, step + REACH)
    needed = stop - start
    own_column = jnp.broadcast_to(own, (BLK, BLK)).T[:, 0:1]
    scale = LOG2E / DH**0.5

    def window(size):
        begin = jnp.minimum(start, step + REACH - size)
        far = jnp.concatenate([labels[begin + t, 0:1, :] for t in range(size)], axis=1).astype(jnp.float32)
        match = own_column == far
        for head in range(PAIR // DH):
            lanes = slice(head * DH, (head + 1) * DH)
            query = query_ref[0, :, lanes]
            key = keys[pl.ds(begin, size), :, lanes].reshape(size * BLK, DH)
            value = values[pl.ds(begin, size), :, lanes].reshape(size * BLK, DH)
            scores = lax.dot_general(query, key, (((1,), (1,)), ((), ())), preferred_element_type=jnp.float32)
            scores = jnp.where(match, scores, -1e30)
            peak = jnp.max(scores, axis=1, keepdims=True)
            expo = jnp.exp2((scores - peak) * scale)
            total = jnp.sum(expo, axis=1, keepdims=True)
            summed = jnp.dot(expo.astype(jnp.bfloat16), value, preferred_element_type=jnp.float32)
            out_ref[0, 0, :, lanes] = (summed / total).astype(jnp.bfloat16)

    smaller = 0
    for size in WINDOWS:
        pl.when((needed > smaller) & (needed <= size))(functools.partial(window, size))
        smaller = size


def attention(here, query, kv):
    return pl.pallas_call(
        attention_body,
        grid_spec=pltpu.PrefetchScalarGridSpec(
            num_scalar_prefetch=1,
            grid=(LINE,),
            in_specs=[pl.BlockSpec((1, BLK, PAIR), lambda i, here: (i, 0, 0))] + [ANY] * 3,
            out_specs=pl.BlockSpec((1, 1, BLK, PAIR), lambda i, here: ((CHIPS - ((i // 2) ^ here[0])) % CHIPS, i % 2, 0, 0)),
            scratch_shapes=[
                pltpu.VMEM((BLOCKS, BLK, PAIR), jnp.bfloat16),
                pltpu.VMEM((BLOCKS, BLK, PAIR), jnp.bfloat16),
                pltpu.VMEM((BLOCKS, MARK, PAIR), jnp.bfloat16),
                pltpu.VMEM((2, BLOCKS, DH), jnp.float32),
                pltpu.SemaphoreType.DMA((9,)),
            ],
        ),
        out_shape=jax.ShapeDtypeStruct((CHIPS, 2, BLK, PAIR), jnp.bfloat16),
        compiler_params=pltpu.CompilerParams(dimension_semantics=("arbitrary",), vmem_limit_bytes=24 * MIB),
        cost_estimate=pl.CostEstimate(flops=2400000000, bytes_accessed=9 * MIB, transcendentals=4700000),
        name="attention",
    )(here, query, *kv)


def project_body(place_ref, own_ref, got_ref, hidden_ref, matrix_ref, out_ref, rows_ref, rest_ref, total_ref, sems):
    columns = out_ref.shape[1]
    copies = []
    for n in range(LINE):
        first = pl.multiple_of(place_ref[1 + n] * PAIR, PAIR)
        copies.append(pltpu.make_async_copy(matrix_ref.at[pl.ds(first, PAIR)], rows_ref.at[n], sems.at[n]))
    first = pl.multiple_of(place_ref[0] * columns, columns)
    rest = pltpu.make_async_copy(hidden_ref.at[:, pl.ds(first, columns)], rest_ref, sems.at[LINE])
    for copy in (*copies, rest):
        copy.start()
    for first in range(0, LINE, 2):
        for n in (first, first + 1):
            copies[n].wait()
        if first == LINE - 2:
            rest.wait()
        rows = [own_ref[n] if n < CHIPS else got_ref[n - CHIPS] for n in (first, first + 1)]
        for at in range(0, columns, PAIR):
            lanes = slice(at, at + PAIR)
            product = jnp.dot(rows[0], rows_ref[first, :, lanes], preferred_element_type=jnp.float32)
            product += jnp.dot(rows[1], rows_ref[first + 1, :, lanes], preferred_element_type=jnp.float32)
            if first == 0:
                total_ref[:, lanes] = product
            elif first < LINE - 2:
                total_ref[:, lanes] += product
            else:
                total = rest_ref[:, lanes].astype(jnp.float32) + (total_ref[:, lanes] + product)
                out_ref[:, lanes] = total.astype(jnp.bfloat16)


def project(place, attended, hidden, matrix):
    columns = matrix.shape[1]
    return pl.pallas_call(
        project_body,
        in_specs=[SCALARS, WHOLE, WHOLE, ANY, ANY],
        out_specs=WHOLE,
        scratch_shapes=[
            pltpu.VMEM((LINE, PAIR, columns), jnp.bfloat16),
            pltpu.VMEM((BLK, columns), jnp.bfloat16),
            pltpu.VMEM((BLK, columns), jnp.float32),
            pltpu.SemaphoreType.DMA((LINE + 1,)),
        ],
        out_shape=jax.ShapeDtypeStruct((BLK, columns), jnp.bfloat16),
        compiler_params=pltpu.CompilerParams(vmem_limit_bytes=60 * MIB),
        cost_estimate=pl.CostEstimate(flops=2, bytes_accessed=2, transcendentals=0),
        name="project",
    )(place, *attended, hidden, matrix)


def after(value, *others):
    return lax.optimization_barrier((value, *others))[0]


def to_next_section(value):
    return lax.ppermute(value, ("x", "zh"), [(s, (s + 1) % 8) for s in range(8)])


def to_other_core(value):
    return lax.ppermute(value, "c", [(0, 1), (1, 0)])


def across(pieces):
    far = [lax.ppermute(piece, "zl", [(z, z ^ MASKS[k]) for z in range(CHIPS)]) for k, piece in enumerate(pieces) if k]
    return [pieces[0], *far]


def on_device(hidden, query, keyv, value, segments, out_weight):
    core, chip = lax.axis_index("c"), lax.axis_index("zl")
    here = jnp.stack([chip, core]).astype(jnp.int32)
    hidden, weight = hidden[0], out_weight[0]
    half = hidden.shape[1] // 2
    part = half // PARTS

    kv, kv_other = pack(here, keyv[0], value[0], segments)
    kv_out = combine(kv, to_other_core(kv_other))
    heads, heads_other = pack(here, query[0])
    heads_out = combine(heads, to_other_core(heads_other))

    rows = [lax.dynamic_slice_in_dim(weight, which * half, half, 1) for which in (core, 1 - core)]
    rows[1] = to_other_core(rows[1])
    rows = [jnp.where(core == place, *rows) for place in (0, 1)]
    rows = [jnp.concatenate([row[:, p * part : (p + 1) * part] for row in rows], axis=0) for p in range(PARTS)]

    def gather(piece, axis):
        return lax.all_gather(piece, axis, axis=0, tiled=True)

    first, second = gather(rows[0], "zl"), gather(rows[1], "zl")
    kv_far = across(kv_out)
    kv_far[2] = after(kv_far[2], *heads_out)
    heads_far = across(heads_out)
    kv = assemble(here, kv_far)
    first = gather(after(first, kv), "y")
    left = lax.ppermute(kv[LINE - SPAN :], "y", [(i, i + 1) for i in range(3)])
    right = lax.ppermute(kv[:SPAN], "y", [(i + 1, i) for i in range(3)])
    heads = assemble(here, heads_far)
    second = gather(after(second, left, right, *heads_far), "y")

    attended = attention(here, heads, (left, kv, right))
    far = across([attended[k] for k in range(CHIPS)])
    first = after(first, *far)
    own, send = divide(here, attended, far[1:])
    attended = [own, to_other_core(send)]

    out = jnp.zeros(hidden.shape, hidden.dtype)
    chips = chip ^ jnp.array(MASKS, jnp.int32)
    order = jnp.concatenate([2 * chips + core, 2 * chips + 1 - core])
    made, arrived = [], []
    for p, matrix in enumerate((first, second)):
        matrix = after(matrix, *attended, *made[-1:], *arrived[-2:-1])
        for which, matrix in ((core, matrix), (1 - core, to_other_core(matrix))):
            place = jnp.concatenate([(which * PARTS + p)[None], order]).astype(jnp.int32)
            ready = [after(rows, *made[-1:], *arrived[-2:-1]) for rows in attended]
            made.append(project(place, ready, hidden, matrix))
            arrived.append(to_next_section(made[-1]))
            out = lax.dynamic_update_slice(out, arrived[-1], (0, which * half + p * part))
    return out[None]


def solution(mesh):
    wide = Mesh(mesh.devices.reshape(4, 2, 4, 4, 2), ("x", "zh", "y", "zl", "c"))
    section, ctx = ("x", "zh"), ("y", "zl", "c")
    return jax.shard_map(
        on_device,
        mesh=wide,
        in_specs=(
            P(section, ctx, None),
            P(section, ctx, None),
            P(section, ctx, None),
            P(section, ctx, None),
            P(section, ctx),
            P(section, ctx, None),
        ),
        out_specs=P(section, ctx, None),
        check_vma=False,
    )
```

```python
import functools

import jax
import jax.numpy as jnp
from jax import lax
from jax.experimental import pallas as pl
from jax.experimental.pallas import tpu as pltpu
from jax.sharding import Mesh, PartitionSpec as P

DH = 128
SPAN = 3
BLK = 256
LINE = 8
PAIR = 256
REACH = 2 * SPAN + 1
BLOCKS = LINE + 2 * SPAN
MARK = 16
LOG2E = 1.4426950408889634
WINDOWS = (2, 3, 4, 5, 7)
PARTS = (1280, 768)
LANE = 128
CHIPS = LINE // 2
MIB = 1024 * 1024


ANY = pl.BlockSpec(memory_space=pl.ANY)
WHOLE = pl.BlockSpec(memory_space=pltpu.VMEM)
SCALARS = pl.BlockSpec(memory_space=pltpu.SMEM)


def run_copies(pairs, sems):
    copies = [pltpu.make_async_copy(src, dst, sems.at[index]) for index, (src, dst) in enumerate(pairs)]
    for copy in copies:
        copy.start()
    for copy in copies:
        copy.wait()


def pack_body(here_ref, *refs):
    arrays, mine_ref, other_ref = refs[:-2], refs[-2], refs[-1]
    chip, core = here_ref[0], here_ref[1]
    for j in range(LINE):

        def store(out_ref, j=j):
            for index, ref in enumerate(arrays):
                if ref.shape[0] == BLK:
                    piece = ref[:, j * PAIR : (j + 1) * PAIR]
                    out_ref[(j // 2) ^ chip, index * BLK : (index + 1) * BLK] = piece
                else:
                    labels = (ref[...] + 1).astype(jnp.float32)
                    out_ref[(j // 2) ^ chip, index * BLK :] = jnp.broadcast_to(labels, (MARK, BLK)).astype(jnp.bfloat16)

        pl.when(core == j % 2)(functools.partial(store, mine_ref))
        pl.when(core != j % 2)(functools.partial(store, other_ref))


def pack(here, *arrays):
    height = sum(BLK if array.shape[0] == BLK else MARK for array in arrays)
    out = jax.ShapeDtypeStruct((CHIPS, height, PAIR), jnp.bfloat16)
    return pl.pallas_call(
        pack_body,
        in_specs=[SCALARS] + [WHOLE] * len(arrays),
        out_specs=[WHOLE, WHOLE],
        out_shape=[out, out],
        compiler_params=pltpu.CompilerParams(vmem_limit_bytes=16 * MIB),
        cost_estimate=pl.CostEstimate(flops=0, bytes_accessed=2 * MIB, transcendentals=0),
        name="pack",
    )(here, *arrays)


def combine_body(mine_ref, got_ref, *refs):
    outs, sems = refs[:-1], refs[-1]
    run_copies([(ref.at[k], out.at[s]) for k, out in enumerate(outs) for s, ref in enumerate((mine_ref, got_ref))], sems)


def combine(mine, got):
    out = jax.ShapeDtypeStruct((2, *mine.shape[1:]), jnp.bfloat16)
    return pl.pallas_call(
        combine_body,
        in_specs=[ANY] * 2,
        out_specs=[pl.BlockSpec(memory_space=pltpu.HBM)] * CHIPS,
        out_shape=[out] * CHIPS,
        scratch_shapes=[pltpu.SemaphoreType.DMA((LINE,))],
        compiler_params=pltpu.CompilerParams(vmem_limit_bytes=4 * MIB),
        cost_estimate=pl.CostEstimate(flops=0, bytes_accessed=2 * MIB, transcendentals=0),
        name="combine",
    )(mine, got)


def assemble_body(here_ref, *refs):
    far, out_ref, sems = refs[:-2], refs[-2], refs[-1]
    chip, core = here_ref[0], here_ref[1]
    pairs = []
    for k, ref in enumerate(far):
        place = 2 * (chip ^ k)
        pairs += [(ref.at[0], out_ref.at[place + core]), (ref.at[1], out_ref.at[place + 1 - core])]
    run_copies(pairs, sems)


def assemble(here, far):
    return pl.pallas_call(
        assemble_body,
        in_specs=[SCALARS] + [ANY] * CHIPS,
        out_specs=ANY,
        out_shape=jax.ShapeDtypeStruct((LINE, *far[0].shape[1:]), jnp.bfloat16),
        scratch_shapes=[pltpu.SemaphoreType.DMA((LINE,))],
        compiler_params=pltpu.CompilerParams(vmem_limit_bytes=4 * MIB),
        cost_estimate=pl.CostEstimate(flops=0, bytes_accessed=2 * MIB, transcendentals=0),
        name="assemble",
    )(here, *far)


def divide_body(here_ref, near_ref, *refs):
    far, own_ref, send_ref, sems = refs[:-3], refs[-3], refs[-2], refs[-1]
    core = here_ref[1]
    pairs = []
    for k, ref in enumerate((near_ref.at[0], *far)):
        pairs += [(ref.at[core], own_ref.at[k]), (ref.at[1 - core], send_ref.at[k])]
    run_copies(pairs, sems)


def divide(here, near, far):
    out = jax.ShapeDtypeStruct((CHIPS, BLK, PAIR), jnp.bfloat16)
    return pl.pallas_call(
        divide_body,
        in_specs=[SCALARS] + [ANY] * CHIPS,
        out_specs=[ANY, ANY],
        out_shape=[out, out],
        scratch_shapes=[pltpu.SemaphoreType.DMA((LINE,))],
        compiler_params=pltpu.CompilerParams(vmem_limit_bytes=4 * MIB),
        cost_estimate=pl.CostEstimate(flops=0, bytes_accessed=2 * MIB, transcendentals=0),
        name="divide",
    )(here, near, *far)


def attention_body(here_ref, query_ref, left_ref, kv_ref, right_ref, out_ref, keys, values, labels, bounds, sems):
    step = pl.program_id(0)

    @pl.when(step == 0)
    def _():
        pairs = []
        for dst, first, rows in ((keys, 0, BLK), (values, BLK, BLK), (labels, 2 * BLK, MARK)):
            at = 0
            for src, count in ((left_ref, SPAN), (kv_ref, LINE), (right_ref, SPAN)):
                pairs.append((src.at[:, pl.ds(first, rows)], dst.at[pl.ds(at, count)]))
                at += count
        run_copies(pairs, sems)

        marks = jnp.max(labels[...].astype(jnp.float32), axis=1)
        top, low = jnp.max(marks, axis=1, keepdims=True), jnp.min(marks, axis=1, keepdims=True)
        place = lax.broadcasted_iota(jnp.int32, (BLOCKS, 1), 0)
        beyond = (place >= SPAN + LINE) & (top == 0.0)
        for index, value in enumerate((top, low)):
            bounds[index] = jnp.broadcast_to(jnp.where(beyond, 99.0, value), (BLOCKS, DH))

    own = jnp.max(labels[step + SPAN].astype(jnp.float32), axis=0, keepdims=True)
    before = bounds[0] < jnp.min(own, axis=1, keepdims=True)
    until = bounds[1] <= jnp.max(own, axis=1, keepdims=True)
    counts = jnp.sum(jnp.where(before, 16.0, 0.0) + jnp.where(until, 1.0, 0.0), axis=0, keepdims=True)
    both = jnp.max(counts).astype(jnp.int32)
    start, stop = jnp.maximum(both // 16, step), jnp.minimum(both % 16, step + REACH)
    needed = stop - start
    own_column = jnp.broadcast_to(own, (BLK, BLK)).T[:, 0:1]
    scale = LOG2E / DH**0.5

    def window(size):
        begin = jnp.minimum(start, step + REACH - size)
        far = jnp.concatenate([labels[begin + t, 0:1, :] for t in range(size)], axis=1).astype(jnp.float32)
        match = own_column == far
        for head in range(PAIR // DH):
            lanes = slice(head * DH, (head + 1) * DH)
            query = query_ref[0, :, lanes]
            key = keys[pl.ds(begin, size), :, lanes].reshape(size * BLK, DH)
            value = values[pl.ds(begin, size), :, lanes].reshape(size * BLK, DH)
            scores = lax.dot_general(query, key, (((1,), (1,)), ((), ())), preferred_element_type=jnp.float32)
            scores = jnp.where(match, scores, -1e30)
            peak = jnp.max(scores, axis=1, keepdims=True)
            expo = jnp.exp2((scores - peak) * scale)
            total = jnp.sum(expo, axis=1, keepdims=True)
            summed = jnp.dot(expo.astype(jnp.bfloat16), value, preferred_element_type=jnp.float32)
            out_ref[0, 0, :, lanes] = (summed / total).astype(jnp.bfloat16)

    smaller = 0
    for size in WINDOWS:
        pl.when((needed > smaller) & (needed <= size))(functools.partial(window, size))
        smaller = size


def attention(here, query, kv):
    return pl.pallas_call(
        attention_body,
        grid_spec=pltpu.PrefetchScalarGridSpec(
            num_scalar_prefetch=1,
            grid=(LINE,),
            in_specs=[pl.BlockSpec((1, BLK, PAIR), lambda i, here: (i, 0, 0))] + [ANY] * 3,
            out_specs=pl.BlockSpec((1, 1, BLK, PAIR), lambda i, here: ((i // 2) ^ here[0], i % 2, 0, 0)),
            scratch_shapes=[
                pltpu.VMEM((BLOCKS, BLK, PAIR), jnp.bfloat16),
                pltpu.VMEM((BLOCKS, BLK, PAIR), jnp.bfloat16),
                pltpu.VMEM((BLOCKS, MARK, PAIR), jnp.bfloat16),
                pltpu.VMEM((2, BLOCKS, DH), jnp.float32),
                pltpu.SemaphoreType.DMA((9,)),
            ],
        ),
        out_shape=jax.ShapeDtypeStruct((CHIPS, 2, BLK, PAIR), jnp.bfloat16),
        compiler_params=pltpu.CompilerParams(dimension_semantics=("arbitrary",), vmem_limit_bytes=24 * MIB),
        cost_estimate=pl.CostEstimate(flops=2400000000, bytes_accessed=9 * MIB, transcendentals=4700000),
        name="attention",
    )(here, query, *kv)


def project_body(place_ref, own_ref, got_ref, hidden_ref, matrix_ref, out_ref, rows_ref, rest_ref, total_ref, sems):
    columns = out_ref.shape[1]
    copies = []
    for n in range(LINE):
        first = pl.multiple_of(place_ref[1 + n] * PAIR, PAIR)
        copies.append(pltpu.make_async_copy(matrix_ref.at[pl.ds(first, PAIR)], rows_ref.at[n], sems.at[n]))
    first = pl.multiple_of(place_ref[0] * LANE, LANE)
    rest = pltpu.make_async_copy(hidden_ref.at[:, pl.ds(first, columns)], rest_ref, sems.at[LINE])
    for copy in (*copies, rest):
        copy.start()
    for first in range(0, LINE, 2):
        for n in (first, first + 1):
            copies[n].wait()
        if first == LINE - 2:
            rest.wait()
        rows = [own_ref[n] if n < CHIPS else got_ref[n - CHIPS] for n in (first, first + 1)]
        for at in range(0, columns, PAIR):
            lanes = slice(at, at + PAIR)
            product = jnp.dot(rows[0], rows_ref[first, :, lanes], preferred_element_type=jnp.float32)
            product += jnp.dot(rows[1], rows_ref[first + 1, :, lanes], preferred_element_type=jnp.float32)
            if first == 0:
                total_ref[:, lanes] = product
            elif first < LINE - 2:
                total_ref[:, lanes] += product
            else:
                total = rest_ref[:, lanes].astype(jnp.float32) + (total_ref[:, lanes] + product)
                out_ref[:, lanes] = total.astype(jnp.bfloat16)


def project(place, attended, hidden, matrix):
    columns = matrix.shape[1]
    return pl.pallas_call(
        project_body,
        in_specs=[SCALARS, WHOLE, WHOLE, ANY, ANY],
        out_specs=WHOLE,
        scratch_shapes=[
            pltpu.VMEM((LINE, PAIR, columns), jnp.bfloat16),
            pltpu.VMEM((BLK, columns), jnp.bfloat16),
            pltpu.VMEM((BLK, columns), jnp.float32),
            pltpu.SemaphoreType.DMA((LINE + 1,)),
        ],
        out_shape=jax.ShapeDtypeStruct((BLK, columns), jnp.bfloat16),
        compiler_params=pltpu.CompilerParams(vmem_limit_bytes=60 * MIB),
        cost_estimate=pl.CostEstimate(flops=2, bytes_accessed=2, transcendentals=0),
        name="project",
    )(place, *attended, hidden, matrix)


def after(value, *others):
    return lax.optimization_barrier((value, *others))[0]


def to_next_section(value):
    return lax.ppermute(value, ("x", "zh"), [(s, (s + 1) % 8) for s in range(8)])


def to_other_core(value):
    return lax.ppermute(value, "c", [(0, 1), (1, 0)])


def across(pieces):
    far = [lax.ppermute(piece, "zl", [(z, z ^ k) for z in range(CHIPS)]) for k, piece in enumerate(pieces) if k]
    return [pieces[0], *far]


def on_device(hidden, query, keyv, value, segments, out_weight):
    core, chip = lax.axis_index("c"), lax.axis_index("zl")
    here = jnp.stack([chip, core]).astype(jnp.int32)
    hidden, weight = hidden[0], out_weight[0]
    half = hidden.shape[1] // 2
    begins = (0, PARTS[0])

    kv, kv_other = pack(here, keyv[0], value[0], segments)
    kv_out = combine(kv, to_other_core(kv_other))
    heads, heads_other = pack(here, query[0])
    heads_out = combine(heads, to_other_core(heads_other))

    rows = [lax.dynamic_slice_in_dim(weight, which * half, half, 1) for which in (core, 1 - core)]
    rows[1] = to_other_core(rows[1])
    rows = [jnp.where(core == place, *rows) for place in (0, 1)]
    rows = [jnp.concatenate([row[:, at : at + part] for row in rows], axis=0) for at, part in zip(begins, PARTS)]

    def gather(piece, axis):
        return lax.all_gather(piece, axis, axis=0, tiled=True)

    first, second = gather(rows[0], "zl"), gather(rows[1], "zl")
    kv_far = across(kv_out)
    kv_far[2] = after(kv_far[2], *heads_out)
    heads_far = across(heads_out)
    kv = assemble(here, kv_far)
    first = gather(after(first, kv), "y")
    left = lax.ppermute(kv[LINE - SPAN :], "y", [(i, i + 1) for i in range(3)])
    right = lax.ppermute(kv[:SPAN], "y", [(i + 1, i) for i in range(3)])
    heads = assemble(here, heads_far)
    second = gather(after(second, left, right, *heads_far), "y")

    attended = attention(here, heads, (left, kv, right))
    far = across([attended[k] for k in range(CHIPS)])
    first = after(first, *far)
    own, send = divide(here, attended, far[1:])
    attended = [own, to_other_core(send)]

    out = jnp.zeros(hidden.shape, hidden.dtype)
    chips = chip ^ jnp.arange(CHIPS, dtype=jnp.int32)
    order = jnp.concatenate([2 * chips + core, 2 * chips + 1 - core])
    made, arrived = [], []
    for begin, matrix in zip(begins, (first, second)):
        matrix = after(matrix, *attended, *made[-1:], *arrived[-2:-1])
        for which, matrix in ((core, matrix), (1 - core, to_other_core(matrix))):
            place = jnp.concatenate([((which * half + begin) // LANE)[None], order]).astype(jnp.int32)
            ready = [after(rows, *made[-1:], *arrived[-2:-1]) for rows in attended]
            made.append(project(place, ready, hidden, matrix))
            arrived.append(to_next_section(made[-1]))
            out = lax.dynamic_update_slice(out, arrived[-1], (0, which * half + begin))
    return out[None]


def solution(mesh):
    wide = Mesh(mesh.devices.reshape(4, 2, 4, 4, 2), ("x", "zh", "y", "zl", "c"))
    section, ctx = ("x", "zh"), ("y", "zl", "c")
    return jax.shard_map(
        on_device,
        mesh=wide,
        in_specs=(
            P(section, ctx, None),
            P(section, ctx, None),
            P(section, ctx, None),
            P(section, ctx, None),
            P(section, ctx),
            P(section, ctx, None),
        ),
        out_specs=P(section, ctx, None),
        check_vma=False,
    )
```
